128 devices in a mesh: req: 4 (over z_hi, core), ctx: 32 (over x, y, z_lo).
Axes of the slice: x: 4, y: 4, z: 4 (z_hi: 2, z_lo: 2; z = z_hi * 2 + z_lo), core: 2. Of those that a mesh axis runs over, the one named last changes fastest.
Arguments:
- queries: bfloat16 [4, 4096, 8192], P('req', 'ctx'), may hold values from -30 to 30
- stretch_kv: bfloat16 [4, 4096, 2048], P('req', 'ctx'), may hold values from -13 to 13
- page_pool: bfloat16 [256, 16, 2048], P(('req', 'ctx')), may hold values from -6 to 6
- slot_owner: int32 [256], replicated, may hold values from 0 to 3, as said below
- slot_fill: int32 [256], replicated, may hold values from 1 to 16
Outputs:
- attended: bfloat16 [4, 4096, 8192], P('req', 'ctx')
The draws below stay inside these ranges and needn't reach their ends.
Inputs may be any that keep to these rules, and one draw needn't show every extreme that they name: `slot_owner`: store device s (numbered along req, then ctx) holds slots s * 2 to s * 2 + 1; they hold 1 pages each of two different requests. In every draw all store devices of some ctx index hold pages of the same two requests.
All inputs are finite; a program needn't handle non-finite values.
Results may differ from the reference program's by a relative error of at most 0.0095.
Values may be sent and summed in bfloat16 or wider, within the bound.
A program may use at most 192 MiB of HBM per device.

```python
import math
import jax
import jax.numpy as jnp
from jax import lax

HEADS = 64
KV_HEADS = 8
HEAD_DIM = 128
PAGE = 16
CAP = 1
PAGES_DEV = 2
REQS = 4
STRETCH = 4096
SLOTS = 256
KV_WIDTH = 2048
N_REQ = 4
N_CTX = 32
DEVICES = 128


def draw_queries(key, part):
    key = jax.random.fold_in(key, 1)
    key_main = jax.random.fold_in(key, 0)
    sampled = jnp.clip(jax.random.normal(key_main, (REQS, STRETCH, HEADS * HEAD_DIM), jnp.float32), -4.0, 4.0)
    return sampled.astype(jnp.bfloat16)


def draw_stretch_kv(key, part):
    key = jax.random.fold_in(key, 2)
    key_main = jax.random.fold_in(key, 0)
    sampled = jnp.clip(jax.random.normal(key_main, (REQS, STRETCH, 2 * KV_HEADS * HEAD_DIM), jnp.float32), -4.0, 4.0)
    return sampled.astype(jnp.bfloat16)


def draw_slot_owner(key, part):
    key = jax.random.fold_in(key, 3)
    key_first, key_second, key_column, key_order = jax.random.split(key, 4)
    first_req = jax.random.randint(key_first, (DEVICES,), 0, N_REQ)
    second_req = (first_req + jax.random.randint(key_second, (DEVICES,), 1, N_REQ)) % N_REQ
    column = jax.random.randint(key_column, (), 0, N_CTX)
    column_of = jnp.arange(DEVICES) % N_CTX
    shared_first = first_req[column]
    shared_second = second_req[column]
    first_req = jnp.where(column_of == column, shared_first, first_req)
    second_req = jnp.where(column_of == column, shared_second, second_req)
    owners = jnp.concatenate([jnp.repeat(first_req[:, None], CAP, axis=1), jnp.repeat(second_req[:, None], CAP, axis=1)], axis=1)
    scores = jax.random.randint(key_order, (DEVICES, PAGES_DEV), 0, 1 << 20) * PAGES_DEV + jnp.arange(PAGES_DEV)[None, :]
    slot_order = jnp.argsort(scores, axis=1)
    owners = jnp.take_along_axis(owners, slot_order, axis=1)
    return owners.reshape(-1).astype(jnp.int32)


def set_ends(result, rng, smallest, largest):
    longest = result.shape.index(max(result.shape))
    spots = []
    for shift in (0, 1):
        where = [jax.random.randint(jax.random.fold_in(rng, axis), (), 0, length) for axis, length in enumerate(result.shape)]
        where[longest] = (where[longest] + shift) % result.shape[longest]
        spots.append(tuple(where))
    return result.at[spots[0]].set(smallest).at[spots[1]].set(largest)


def level_of(stream_key, dims, shards, least, high):
    def one(axis_at, shards_of):
        heights = jax.random.uniform(jax.random.fold_in(jax.random.fold_in(stream_key, 6), axis_at), (shards_of,), jnp.float32, least / len(shards), high / len(shards))
        return jnp.repeat(jnp.exp(heights), dims[axis_at] // shards_of).reshape((-1,) + (1,) * (len(dims) - axis_at - 1))

    level = one(*shards[0])
    for cut in shards[1:]:
        level = level * one(*cut)
    return level


def noise(own_key, dims, width, limit, cuts=(), held_as=jnp.bfloat16):
    result = jax.random.normal(own_key, dims, jnp.float32) * width
    if len(cuts) > 0:
        result = level_of(own_key, dims, cuts, -0.22, 0.18) * result
    return jnp.clip(result, min=-limit, max=limit).astype(held_as)


def setup_inputs(seed: int = 0) -> dict:
    keys = jax.random.split(jax.random.key(seed), 6)
    return {
        "queries": draw_queries(jax.random.fold_in(keys[5], 71), 0),
        "stretch_kv": draw_stretch_kv(jax.random.fold_in(keys[5], 71), 0),
        "page_pool": noise(keys[2], (SLOTS, PAGE, KV_WIDTH), 1.0, 6.0, ((0, 128),)),
        "slot_owner": draw_slot_owner(jax.random.fold_in(keys[5], 71), 0),
        "slot_fill": set_ends(jax.random.randint(keys[4], (SLOTS,), 1, PAGE + 1), jax.random.fold_in(keys[4], 1), 1, PAGE).astype(jnp.int32),
    }


masked_score = -1.0e30


def reference(queries, stretch_kv, page_pool, slot_owner, slot_fill):
    score_scale = HEAD_DIM ** -0.5
    slot_limit = DEVICES * CAP
    group_size = HEADS // KV_HEADS
    half_width = KV_HEADS * HEAD_DIM
    block_rows = math.gcd(STRETCH, 512)
    results = []
    for request in range(REQS):
        slot_order = jnp.argsort((slot_owner != request).astype(jnp.int32), stable=True)[:slot_limit]
        is_owned = slot_owner[slot_order] == request
        within = jnp.arange(PAGE, dtype=jnp.int32)
        usable = is_owned[:, None] & (within[None, :] < slot_fill[slot_order][:, None])
        prefix = page_pool[slot_order].reshape(slot_limit * PAGE, KV_WIDTH)
        keys_all = jnp.concatenate([prefix, stretch_kv[request]], axis=0)
        usable_all = jnp.concatenate([usable.reshape(-1), jnp.ones((STRETCH,), dtype=bool)])
        key_pos = jnp.concatenate([jnp.full((slot_limit * PAGE,), -1, dtype=jnp.int32), jnp.arange(STRETCH, dtype=jnp.int32)])
        key_rows = keys_all[:, :half_width].reshape(-1, KV_HEADS, HEAD_DIM).astype(jnp.float32).transpose(1, 0, 2)
        value_rows = keys_all[:, half_width:].reshape(-1, KV_HEADS, HEAD_DIM).astype(jnp.float32).transpose(1, 0, 2)
        query_heads = queries[request].reshape(STRETCH // block_rows, block_rows, KV_HEADS, group_size, HEAD_DIM)
        block_start = jnp.arange(STRETCH // block_rows, dtype=jnp.int32) * block_rows

        def attend_block(inputs):
            query_block, first_row = inputs
            query_pos = first_row + jnp.arange(block_rows, dtype=jnp.int32)
            visible = (key_pos[None, :] <= query_pos[:, None]) & usable_all[None, :]

            def per_group(group_inputs):
                query_group, key_group, value_group = group_inputs
                scores = jnp.einsum("tgd,jd->gtj", query_group.astype(jnp.float32), key_group) * score_scale
                scores = jnp.where(visible[None], scores, masked_score)
                top_score = jnp.max(scores, axis=-1, keepdims=True)
                weights = jnp.where(visible[None], jnp.exp(scores - top_score), 0.0).astype(jnp.bfloat16)
                norm_sum = jnp.sum(weights.astype(jnp.float32), axis=-1)
                mixed = jnp.einsum("gtj,jd->gtd", weights.astype(jnp.float32), value_group)
                return (mixed / norm_sum[..., None]).astype(jnp.bfloat16)

            grouped = lax.map(per_group, (query_block.transpose(1, 0, 2, 3), key_rows, value_rows))
            return grouped.transpose(2, 0, 1, 3).reshape(block_rows, HEADS * HEAD_DIM)

        attended = lax.map(attend_block, (query_heads, block_start)).reshape(STRETCH, HEADS * HEAD_DIM)
        results.append(attended)
    return jnp.stack(results)
```

```python
import functools

import jax
import jax.numpy as jnp
from jax import lax
from jax.experimental import pallas as pl
from jax.experimental.pallas import tpu as pltpu
from jax.sharding import PartitionSpec as P

HEAD_DIM = 128
GROUP_HEADS = 8
KEY_HEADS = 2
ROWS = 128
N_REQ = 4
N_CTX = 32
PAGE = 16
CHUNK = 512
LOW = -1e30
SCALE = HEAD_DIM ** -0.5 * 1.4426950408889634
MESH = pl.DeviceIdType.MESH
Q_COLS = KEY_HEADS * GROUP_HEADS * HEAD_DIM
K_COLS = KEY_HEADS * HEAD_DIM
KV_COLS = 2 * K_COLS
V_AT = 1024
COMPUTE = True


def kernel(owner, fill, q_hbm, kv_hbm, pages, out_hbm, qbuf, kvbuf, pbuf, page_out, page_in, obuf, pbias,
           qs, acc, top, page_sems, gkv_sems, gq_sems, gp_sems, ckv_sems, cp_sems, o_sems, own_sems):
    req = lax.axis_index("req")
    ctx = lax.axis_index("ctx")
    x, y, z = ctx // 8, (ctx // 2) % 4, ctx % 2

    def place(cube, group):
        cube_x, cube_y, cube_z = cube % 2, (cube // 2) % 2, cube // 4
        group_x, group_y = group % 2, group // 2
        px = x + cube_x * (1 - 2 * (x % 2))
        py = y + cube_y * (1 - 2 * (y % 2))
        pz = z + cube_z * (1 - 2 * z)
        px = px + group_x * (3 - 2 * px)
        py = py + group_y * (3 - 2 * py)
        return px * 8 + py * 2 + pz

    def quarter(group):
        half_x, half_y = x // 2, y // 2
        half_x = half_x + (group % 2) * (1 - 2 * half_x)
        half_y = half_y + (group // 2) * (1 - 2 * half_y)
        return half_x * 2 + half_y

    def cols(start, size):
        return pl.ds(pl.multiple_of(start, 128), size)

    def remote(src, dst, sems, index, ctx_to, req_to=None):
        return pltpu.make_async_remote_copy(
            src_ref=src, dst_ref=dst, send_sem=sems.at[0, index], recv_sem=sems.at[1, index],
            device_id=(req if req_to is None else req_to, ctx_to), device_id_type=MESH)

    barrier = pltpu.get_barrier_semaphore()
    for step in range(1, N_REQ):
        pl.semaphore_signal(barrier, inc=1, device_id=((req + step) % N_REQ, ctx), device_id_type=MESH)
    for group in range(1, 4):
        pl.semaphore_signal(barrier, inc=1, device_id=(req, place(0, group)), device_id_type=MESH)
    for cube in (1, 2, 4):
        pl.semaphore_signal(barrier, inc=1, device_id=(req, place(cube, 0)), device_id_type=MESH)

    first_slot = (req * N_CTX + ctx) * 2
    for target in range(N_REQ):
        picked = jnp.where(owner[first_slot] == target, 0, 1)
        page_out[target] = pages[picked]
    page_in[pl.ds(req * PAGE, PAGE)] = page_out[req]
    mine = quarter(0)
    own_copies = [
        pltpu.make_async_copy(kv_hbm.at[0, :, cols(mine * K_COLS, K_COLS)], kvbuf.at[ctx, :, 0:K_COLS], own_sems.at[0]),
        pltpu.make_async_copy(
            kv_hbm.at[0, :, cols(V_AT + mine * K_COLS, K_COLS)], kvbuf.at[ctx, :, K_COLS:KV_COLS], own_sems.at[1]),
        pltpu.make_async_copy(q_hbm.at[0, :, cols(mine * Q_COLS, Q_COLS)], qbuf.at[0], own_sems.at[2]),
    ]
    for copy in own_copies:
        copy.start()
    pl.semaphore_wait(barrier, 9)

    started = []

    def start(copy):
        copy.start()
        started.append(copy)
        return copy

    page_copies = []
    for step in range(1, N_REQ):
        target = (req + step) % N_REQ
        page_copies.append(start(remote(
            page_out.at[target], page_in.at[pl.ds(req * PAGE, PAGE)], page_sems, step - 1, ctx, target)))
    kv_copies = []
    for group in range(1, 4):
        theirs = quarter(group)
        for part in range(2):
            kv_copies.append(start(remote(
                kv_hbm.at[0, :, cols(part * V_AT + theirs * K_COLS, K_COLS)],
                kvbuf.at[ctx, :, part * K_COLS:(part + 1) * K_COLS],
                gkv_sems, group * 2 + part, place(0, group))))
    q_copies = []
    for group in range(1, 4):
        q_copies.append(start(remote(
            q_hbm.at[0, :, cols(quarter(group) * Q_COLS, Q_COLS)], qbuf.at[group], gq_sems, group, place(0, group))))

    for copy in page_copies:
        copy.wait_recv()
    group_pages = []
    for group in range(1, 4):
        theirs = quarter(group)
        for part in range(2):
            group_pages.append(start(remote(
                page_in.at[:, cols(part * V_AT + theirs * K_COLS, K_COLS)],
                pbuf.at[0, group, :, part * K_COLS:(part + 1) * K_COLS],
                gp_sems, group * 2 + part, place(0, group))))
    pbuf[0, 0, :, 0:K_COLS] = page_in[:, cols(mine * K_COLS, K_COLS)]
    pbuf[0, 0, :, K_COLS:KV_COLS] = page_in[:, cols(V_AT + mine * K_COLS, K_COLS)]

    arriving = {}

    def send_prefix(held, bit):
        arriving["p", held ^ bit] = [start(remote(
            pbuf.at[held], pbuf.at[held ^ bit], cp_sems, held ^ bit, place(bit, 0)))]

    def send_blocks(name, members, held, bit):
        arriving[name, held ^ bit] = [
            start(remote(kvbuf.at[place(held, group)], kvbuf.at[place(held, group)], ckv_sems,
                         (held ^ bit) * 4 + group, place(bit, 0)))
            for group in members]

    orders = {"a": (2, 4, 1), "b": (4, 1, 2), "p": (1, 2, 4)}
    held = {"a": [0], "b": [0], "p": [0]}
    for copy in own_copies[:2]:
        copy.wait()
    for copy in kv_copies:
        copy.wait_recv()
    for step in range(3):
        for name in ("a", "b", "p"):
            if step == 0 and name == "p":
                for copy in group_pages:
                    copy.wait_recv()
            if step > 0:
                for index in held[name]:
                    for copy in arriving.pop((name, index), []):
                        copy.wait_recv()
            bit = orders[name][step]
            for index in held[name]:
                if name == "p":
                    send_prefix(index, bit)
                else:
                    send_blocks(name, (0, 1) if name == "a" else (2, 3), index, bit)
            held[name] = held[name] + [index ^ bit for index in held[name]]

    lane = lax.broadcasted_iota(jnp.int32, (1, 8 * 4 * N_REQ * PAGE), 1)

    def count_page(index, counts):
        source = place(index // 16, (index // 4) % 4)
        slot = ((index % 4) * N_CTX + source) * 2
        written = jnp.where(owner[slot] == req, fill[slot], jnp.where(owner[slot + 1] == req, fill[slot + 1], 0))
        return jnp.where(lane // PAGE == index, written, counts)

    counts = lax.fori_loop(0, 8 * 4 * N_REQ, count_page, jnp.zeros_like(lane))
    pbias[...] = jnp.where(lane % PAGE < counts, 0.0, LOW)

    own_copies[2].wait()
    for copy in q_copies:
        copy.wait_recv()
    for copies in arriving.values():
        for copy in copies:
            copy.wait_recv()

    ones = jnp.ones((CHUNK, HEAD_DIM), jnp.bfloat16)

    def product(head, keys):
        return lax.dot_general(qs[head], keys, (((1,), (1,)), ((), ())), preferred_element_type=jnp.float32)

    def absorb(head, scores, values):
        old = top[head]
        new = jnp.maximum(old, jnp.max(scores, axis=-1, keepdims=True))
        factor = jnp.exp2((old - new) * SCALE)
        weights = jnp.exp2((scores - jnp.tile(new, (1, CHUNK // HEAD_DIM))) * SCALE).astype(jnp.bfloat16)
        summed = jnp.dot(weights, jnp.concatenate([values, ones], axis=1), preferred_element_type=jnp.float32)
        acc[head] = acc[head] * jnp.tile(factor, (1, 2)) + summed
        top[head] = new

    def out_copy(member, slot):
        return remote(obuf.at[member], out_hbm.at[0, :, cols(mine * Q_COLS, Q_COLS)], o_sems, slot, place(0, member))

    def attend(turn, _):
        member = (turn + 1) % 4
        position = place(0, member)
        for head in range(KEY_HEADS):
            for g in range(GROUP_HEADS):
                at = (head * GROUP_HEADS + g) * HEAD_DIM
                qs[head, g * ROWS:(g + 1) * ROWS, :] = qbuf[member, :, at:at + HEAD_DIM]
            acc[head] = jnp.zeros((GROUP_HEADS * ROWS, 2 * HEAD_DIM), jnp.float32)
            top[head] = jnp.full((GROUP_HEADS * ROWS, HEAD_DIM), LOW, jnp.float32)

        def prefix_step(step, _):
            block = pbuf[pl.ds(step * 2, 2)].reshape(CHUNK, KV_COLS)
            bias = pbias[:, pl.ds(pl.multiple_of(step * CHUNK, CHUNK), CHUNK)]
            for head in range(KEY_HEADS):
                at = head * HEAD_DIM
                absorb(head, product(head, block[:, at:at + HEAD_DIM]) + bias,
                       block[:, K_COLS + at:K_COLS + at + HEAD_DIM])
            return 0

        def stretch(step, masked):
            block = kvbuf[pl.ds(step * 4, 4)].reshape(CHUNK, KV_COLS)
            for head in range(KEY_HEADS):
                at = head * HEAD_DIM
                scores = product(head, block[:, at:at + HEAD_DIM])
                if masked:
                    ahead = (lax.broadcasted_iota(jnp.int32, scores.shape, 1)
                             - lax.broadcasted_iota(jnp.int32, scores.shape, 0) % ROWS)
                    scores = jnp.where(ahead <= position * ROWS - step * CHUNK, scores, LOW)
                absorb(head, scores, block[:, K_COLS + at:K_COLS + at + HEAD_DIM])
            return 0

        if COMPUTE:
            lax.fori_loop(0, 4, prefix_step, 0)
            lax.fori_loop(0, position // 4, lambda step, _: stretch(step, False), 0)
            stretch(position // 4, True)
        for head in range(KEY_HEADS):
            result = (acc[head, :, :HEAD_DIM] / acc[head, :, HEAD_DIM:]).astype(jnp.bfloat16)
            for g in range(GROUP_HEADS):
                at = (head * GROUP_HEADS + g) * HEAD_DIM
                obuf[member, :, at:at + HEAD_DIM] = result[g * ROWS:(g + 1) * ROWS]

        @pl.when(turn < 3)
        def _():
            out_copy(member, member).start()

        return 0

    lax.fori_loop(0, 4, attend, 0)
    last = pltpu.make_async_copy(obuf.at[0], out_hbm.at[0, :, cols(mine * Q_COLS, Q_COLS)], own_sems.at[3])
    last.start()
    for member in range(1, 4):
        out_copy(member, member).wait_recv()
    for copy in started:
        copy.wait_send()
    for member in range(1, 4):
        out_copy(member, member).wait_send()
    last.wait()


def shards(queries, stretch_kv, page_pool, slot_owner, slot_fill):
    vmem = pltpu.VMEM
    dma = pltpu.SemaphoreType.DMA
    wide = GROUP_HEADS * ROWS
    smem_spec = pl.BlockSpec(memory_space=pltpu.SMEM)
    any_spec = pl.BlockSpec(memory_space=pl.ANY)
    return pl.pallas_call(
        kernel,
        out_shape=jax.ShapeDtypeStruct(queries.shape, jnp.bfloat16),
        in_specs=[smem_spec, smem_spec, any_spec, any_spec, pl.BlockSpec(memory_space=vmem)],
        out_specs=any_spec,
        scratch_shapes=[
            vmem((4, ROWS, Q_COLS), jnp.bfloat16),
            vmem((N_CTX, ROWS, KV_COLS), jnp.bfloat16),
            vmem((8, 4, N_REQ * PAGE, KV_COLS), jnp.bfloat16),
            vmem((N_REQ, PAGE, 2048), jnp.bfloat16),
            vmem((N_REQ * PAGE, 2048), jnp.bfloat16),
            vmem((4, ROWS, Q_COLS), jnp.bfloat16),
            vmem((1, 8 * 4 * N_REQ * PAGE), jnp.float32),
            vmem((KEY_HEADS, wide, HEAD_DIM), jnp.bfloat16),
            vmem((KEY_HEADS, wide, 2 * HEAD_DIM), jnp.float32),
            vmem((KEY_HEADS, wide, HEAD_DIM), jnp.float32),
            dma((2, 3)),
            dma((2, 8)),
            dma((2, 4)),
            dma((2, 8)),
            dma((2, 32)),
            dma((2, 8)),
            dma((2, 4)),
            dma((4,)),
        ],
        compiler_params=pltpu.CompilerParams(
            collective_id=0, has_side_effects=True, vmem_limit_bytes=56 * 2 ** 20),
        cost_estimate=pl.CostEstimate(flops=18 * 10 ** 9, bytes_accessed=6 * 10 ** 6, transcendentals=40 * 10 ** 6),
    )(slot_owner, slot_fill, queries, stretch_kv, page_pool)


def solution(mesh):
    placed = (P("req", "ctx", None), P("req", "ctx", None), P(("req", "ctx"), None, None), P(), P())
    return jax.shard_map(
        shards, mesh=mesh, in_specs=placed, out_specs=P("req", "ctx", None), check_vma=False
    )
```

```python
import functools

import jax
import jax.numpy as jnp
from jax import lax
from jax.experimental import pallas as pl
from jax.experimental.pallas import tpu as pltpu
from jax.sharding import PartitionSpec as P

HEAD_DIM = 128
GROUP_HEADS = 8
ROWS = 128
MEMBERS = 8
SQUARE = 4
N_REQ = 4
N_CTX = 32
PAGE = 16
V_AT = 1024
CHUNK = 512
ROOM = 768
PREFIX_ROWS = 2048
WIDE = GROUP_HEADS * ROWS
Q_COLS = GROUP_HEADS * HEAD_DIM
LOW = -1e30
SCALE = HEAD_DIM ** -0.5 * 1.4426950408889634
MESH = pl.DeviceIdType.MESH
COMPUTE = True


def kernel(room, owner, fill, q_hbm, kv_hbm, pages, out_hbm, q_own, qbuf, near_kv, far_kv, pbuf, packed, page_out, page_in, obuf,
           pbias, acc, top, held, held_prefix, page_sems, gkv_sems, gq_sems, gp_sems, sq_sems, sp_sems, o_sems, own_sems):
    req = lax.axis_index("req")
    ctx = lax.axis_index("ctx")
    x, y, z = ctx // 8, (ctx // 2) % 4, ctx % 2

    def spot(square, group):
        px = x + (square % 2) * (1 - 2 * (x % 2))
        py = y + (square // 2) * (1 - 2 * (y % 2))
        px = px + (group // 4) * (3 - 2 * px)
        py = py + ((group // 2) % 2) * (3 - 2 * py)
        return px, py, z + (group % 2) * (1 - 2 * z)

    def place(square, group):
        px, py, pz = spot(square, group)
        return px * 8 + py * 2 + pz

    def head_of(group):
        px, py, pz = spot(0, group)
        return (px // 2) * 4 + (py // 2) * 2 + pz

    def cols(start, size):
        return pl.ds(pl.multiple_of(start, 128), size)

    def remote(src, dst, sems, index, ctx_to, req_to=None):
        return pltpu.make_async_remote_copy(
            src_ref=src, dst_ref=dst, send_sem=sems.at[0, index], recv_sem=sems.at[1, index],
            device_id=(req if req_to is None else req_to, ctx_to), device_id_type=MESH)

    barrier = pltpu.get_barrier_semaphore()
    for step in range(1, N_REQ):
        pl.semaphore_signal(barrier, inc=1, device_id=((req + step) % N_REQ, ctx), device_id_type=MESH)
    for group in range(1, MEMBERS):
        pl.semaphore_signal(barrier, inc=1, device_id=(req, place(0, group)), device_id_type=MESH)
    for square in (1, 2):
        pl.semaphore_signal(barrier, inc=1, device_id=(req, place(square, 0)), device_id_type=MESH)

    first_slot = (req * N_CTX + ctx) * 2
    for target in range(N_REQ):
        picked = jnp.where(owner[first_slot] == target, 0, 1)
        page_out[target] = pages[picked]
    page_in[pl.ds(req * PAGE, PAGE)] = page_out[req]
    mine = head_of(0)

    def kv_piece(group, part):
        head = head_of(group)
        return (kv_hbm.at[0, :, cols(part * V_AT + head * HEAD_DIM, HEAD_DIM)],
                near_kv.at[0, group, :, part * HEAD_DIM:(part + 1) * HEAD_DIM])

    def q_copy(group):
        return remote(q_hbm.at[0, :, cols(head_of(group) * Q_COLS, Q_COLS)], qbuf.at[group], gq_sems, group,
                      place(0, group))

    own_kv = [pltpu.make_async_copy(*kv_piece(0, part), own_sems.at[part]) for part in range(2)]
    own_q = pltpu.make_async_copy(q_hbm.at[0, :, cols(mine * Q_COLS, Q_COLS)], q_own, own_sems.at[2])
    for copy in own_kv:
        copy.start()
    own_q.start()
    pl.semaphore_wait(barrier, N_REQ - 1 + MEMBERS - 1 + 2)

    started = []

    def start(copy):
        copy.start()
        started.append(copy)
        return copy

    page_copies = []
    for step in range(1, N_REQ):
        target = (req + step) % N_REQ
        page_copies.append(start(remote(
            page_out.at[target], page_in.at[pl.ds(req * PAGE, PAGE)], page_sems, step - 1, ctx, target)))
    near = (1, 2, 4, 3, 5, 6, 7)
    kv_copies = {0: own_kv}
    for group in near:
        kv_copies[group] = [
            start(remote(*kv_piece(group, part), gkv_sems, group * 2 + part, place(0, group)))
            for part in range(2)]

    for copy in page_copies:
        copy.wait_recv()
    group_pages = []
    for group in near:
        theirs = head_of(group)
        for part in range(2):
            group_pages.append(start(remote(
                page_in.at[:, cols(part * V_AT + theirs * HEAD_DIM, HEAD_DIM)],
                pbuf.at[0, group, :, part * HEAD_DIM:(part + 1) * HEAD_DIM],
                gp_sems, group * 2 + part, place(0, group))))
    for part in range(2):
        pbuf[0, 0, :, part * HEAD_DIM:(part + 1) * HEAD_DIM] = page_in[:, cols(part * V_AT + mine * HEAD_DIM, HEAD_DIM)]

    def pass_block(slot, group, bit):
        source = near_kv.at[slot // 2, group]
        target = (far_kv if bit == 1 else near_kv).at[(slot + bit) // 2, group]
        return start(remote(source, target, sq_sems, (slot + bit) * MEMBERS + group, place(bit, 0)))

    def pass_prefix(slot, bit):
        return start(remote(pbuf.at[slot], pbuf.at[slot + bit], sp_sems, slot + bit, place(bit, 0)))

    blocks = {1: [], 2: [], 3: []}
    for group in (0,) + near:
        for copy in kv_copies[group]:
            copy.wait() if group == 0 else copy.wait_recv()
        blocks[2].append(pass_block(0, group, 2))
        blocks[1].append(pass_block(0, group, 1))
    for copy in group_pages:
        copy.wait_recv()
    prefixes = {1: pass_prefix(0, 1), 2: pass_prefix(0, 2)}
    for group in near:
        start(q_copy(group))

    def product(member, keys, queries_of=None):
        queries_of = qbuf.at[member] if queries_of is None else queries_of
        queries = jnp.concatenate(
            [queries_of[:, g * HEAD_DIM:(g + 1) * HEAD_DIM] for g in range(GROUP_HEADS)], axis=0)
        return lax.dot_general(queries, keys, (((1,), (1,)), ((), ())), preferred_element_type=jnp.float32)

    def weigh(scores, new, values):
        size = scores.shape[1]
        weights = jnp.exp2((scores - jnp.tile(new, (1, size // HEAD_DIM))) * SCALE).astype(jnp.bfloat16)
        ones = jnp.ones((size, HEAD_DIM), jnp.bfloat16)
        return jnp.dot(weights, jnp.concatenate([values, ones], axis=1), preferred_element_type=jnp.float32)

    def begin(member, scores, values):
        new = jnp.broadcast_to(jnp.max(scores, axis=-1, keepdims=True), (WIDE, HEAD_DIM))
        acc[member] = weigh(scores, new, values)
        top[member] = new

    def absorb(member, scores, values):
        old = top[member]
        new = jnp.maximum(old, jnp.max(scores, axis=-1, keepdims=True))
        factor = jnp.exp2((old - new) * SCALE)
        acc[member] = acc[member] * jnp.tile(factor, (1, 2)) + weigh(scores, new, values)
        top[member] = new

    def keys_of(buffer, which, half):
        return buffer[which, pl.ds(half * 4, 4), :, 0:HEAD_DIM].reshape(CHUNK, HEAD_DIM)

    def values_of(buffer, which, half):
        return buffer[which, pl.ds(half * 4, 4), :, HEAD_DIM:2 * HEAD_DIM].reshape(CHUNK, HEAD_DIM)

    def mask(scores, square, member):
        _, py, pz = spot(0, member)
        _, key_y, _ = spot(square, 0)
        lane = lax.broadcasted_iota(jnp.int32, (1, CHUNK), 1)
        from_y, from_z = lane // (2 * ROWS), (lane // ROWS) % 2
        at_y = key_y + from_y * (3 - 2 * key_y)
        at_z = z + from_z * (1 - 2 * z)
        token = (at_y * 2 + at_z - (py * 2 + pz)) * ROWS + lane % ROWS
        row = lax.broadcasted_iota(jnp.int32, (WIDE, 1), 0) % ROWS
        return jnp.where(token <= row, scores, LOW)

    def near_keys(member, queries_of=None):
        px, py, _ = spot(0, member)
        half = member // 4
        held[0] = product(member, keys_of(near_kv, 0, half), queries_of)

        @pl.when(px >= 2)
        def _():
            held[1] = product(member, keys_of(near_kv, 0, 1 - half), queries_of)
            begin(member, mask(held[0], 0, member), values_of(near_kv, 0, half))
            held[0] = product(member, keys_of(near_kv, 1, half), queries_of)
            absorb(member, held[1], values_of(near_kv, 0, 1 - half))
            held[1] = product(member, keys_of(near_kv, 1, 1 - half), queries_of)
            absorb(member, mask(held[0], 2, member), values_of(near_kv, 1, half))
            absorb(member, held[1], values_of(near_kv, 1, 1 - half))

        @pl.when((px < 2) & (py > 0))
        def _():
            held[1] = product(member, keys_of(near_kv, 1, half), queries_of)
            begin(member, mask(held[0], 0, member), values_of(near_kv, 0, half))
            absorb(member, mask(held[1], 2, member), values_of(near_kv, 1, half))

        @pl.when((px < 2) & (py == 0))
        def _():
            begin(member, mask(held[0], 0, member), values_of(near_kv, 0, half))

    def x_half():
        return spot(1, 0)[0] // 3

    row = (lax.broadcasted_iota(jnp.int32, (PAGE, HEAD_DIM), 0) * HEAD_DIM
           + lax.broadcasted_iota(jnp.int32, (PAGE, HEAD_DIM), 1))

    def count_page(index, carry):
        places, before = carry
        source = place(index // (MEMBERS * N_REQ), (index // N_REQ) % MEMBERS)
        slot = ((index % N_REQ) * N_CTX + source) * 2
        written = jnp.where(owner[slot] == req, fill[slot], jnp.where(owner[slot + 1] == req, fill[slot + 1], 0))
        token = row - index * PAGE
        inside = (token >= 0) & (token < written)
        return jnp.where(inside, token + before, places), before + written

    places, total = lax.fori_loop(0, PREFIX_ROWS // PAGE, count_page, (jnp.full_like(row, -1), jnp.int32(0)))
    pbias[...] = jnp.where(lax.broadcasted_iota(jnp.int32, (1, room), 1) < total, 0.0, LOW)

    for group, copy in zip((0,) + near, blocks[2], strict=True):
        copy.wait_recv()
        blocks[3].append(pass_block(2, group, 1))
    prefixes[1].wait_recv()
    prefixes[3] = pass_prefix(1, 2)
    own_q.wait()
    if COMPUTE:
        near_keys(0, q_own)
    qbuf[0] = q_own[...]
    for group in near:
        q_copy(group).wait_recv()
    if COMPUTE:
        lax.fori_loop(1, MEMBERS, lambda member, _: (near_keys(member), 0)[1], 0)

    prefixes[2].wait_recv()
    prefixes[3].wait_recv()
    if COMPUTE:
        for at in range(0, room, 256):
            wanted = lax.broadcasted_iota(jnp.int32, (256, HEAD_DIM), 0) + at
            chosen = jnp.concatenate(
                [jnp.where(wanted == places[k:k + 1], 1.0, 0.0).astype(jnp.bfloat16) for k in range(PAGE)], axis=1)
            packed[at:at + 256] = jnp.dot(
                chosen, pbuf[...].reshape(PREFIX_ROWS, 2 * HEAD_DIM), preferred_element_type=jnp.float32
            ).astype(jnp.bfloat16)

    for copy in blocks[1] + blocks[3]:
        copy.wait_recv()

    def out_copy(member):
        return remote(obuf.at[member], out_hbm.at[0, :, cols(mine * Q_COLS, Q_COLS)], o_sems, member, place(0, member))

    piece = ROOM if room == ROOM else CHUNK

    def prefix_scores(member, at):
        return product(member, packed[at:at + piece, 0:HEAD_DIM]) + pbias[:, at:at + piece]

    def absorb_prefix(member, at, scores):
        absorb(member, scores, packed[at:at + piece, HEAD_DIM:2 * HEAD_DIM])

    def other_keys(turn, _):
        member = MEMBERS - 1 - turn
        px, _, _ = spot(0, member)
        if COMPUTE:
            held_prefix[:, :piece] = prefix_scores(member, 0)

            @pl.when(px == 3)
            def _():
                held[0] = product(member, keys_of(far_kv, 0, 0))
                absorb_prefix(member, 0, held_prefix[:, :piece])
                held[1] = product(member, keys_of(far_kv, 0, 1))
                absorb(member, held[0], values_of(far_kv, 0, 0))
                held[0] = product(member, keys_of(far_kv, 1, 0))
                absorb(member, held[1], values_of(far_kv, 0, 1))
                held[1] = product(member, keys_of(far_kv, 1, 1))
                absorb(member, held[0], values_of(far_kv, 1, 0))
                absorb(member, held[1], values_of(far_kv, 1, 1))

            @pl.when((px == 1) | (px == 2))
            def _():
                half = x_half()
                held[0] = product(member, keys_of(far_kv, 0, half))
                absorb_prefix(member, 0, held_prefix[:, :piece])
                held[1] = product(member, keys_of(far_kv, 1, half))
                absorb(member, held[0], values_of(far_kv, 0, half))
                absorb(member, held[1], values_of(far_kv, 1, half))

            @pl.when(px == 0)
            def _():
                absorb_prefix(member, 0, held_prefix[:, :piece])

            for at in range(piece, room, piece):
                absorb_prefix(member, at, prefix_scores(member, at))
        result = (acc[member, :, :HEAD_DIM] / acc[member, :, HEAD_DIM:]).astype(jnp.bfloat16)
        for g in range(GROUP_HEADS):
            obuf[member, :, g * HEAD_DIM:(g + 1) * HEAD_DIM] = result[g * ROWS:(g + 1) * ROWS]

        @pl.when(member > 0)
        def _():
            out_copy(member).start()

        return 0

    lax.fori_loop(0, MEMBERS, other_keys, 0)
    last_copy = pltpu.make_async_copy(obuf.at[0], out_hbm.at[0, :, cols(mine * Q_COLS, Q_COLS)], own_sems.at[3])
    last_copy.start()
    for copy in started:
        copy.wait_send()
    for member in range(1, MEMBERS):
        out_copy(member).wait_recv()
        out_copy(member).wait_send()
    last_copy.wait()


def attend(room, queries, stretch_kv, page_pool, slot_owner, slot_fill):
    vmem = pltpu.VMEM
    dma = pltpu.SemaphoreType.DMA
    smem_spec = pl.BlockSpec(memory_space=pltpu.SMEM)
    any_spec = pl.BlockSpec(memory_space=pl.ANY)
    return pl.pallas_call(
        functools.partial(kernel, room),
        out_shape=jax.ShapeDtypeStruct(queries.shape, jnp.bfloat16),
        in_specs=[smem_spec, smem_spec, any_spec, any_spec, pl.BlockSpec(memory_space=vmem)],
        out_specs=any_spec,
        scratch_shapes=[
            vmem((ROWS, Q_COLS), jnp.bfloat16),
            vmem((MEMBERS, ROWS, Q_COLS), jnp.bfloat16),
            vmem((SQUARE // 2, MEMBERS, ROWS, 2 * HEAD_DIM), jnp.bfloat16),
            vmem((SQUARE // 2, MEMBERS, ROWS, 2 * HEAD_DIM), jnp.bfloat16),
            vmem((SQUARE, MEMBERS, N_REQ * PAGE, 2 * HEAD_DIM), jnp.bfloat16),
            vmem((room, 2 * HEAD_DIM), jnp.bfloat16),
            vmem((N_REQ, PAGE, 2048), jnp.bfloat16),
            vmem((N_REQ * PAGE, 2048), jnp.bfloat16),
            vmem((MEMBERS, ROWS, Q_COLS), jnp.bfloat16),
            vmem((1, room), jnp.float32),
            vmem((MEMBERS, WIDE, 2 * HEAD_DIM), jnp.float32),
            vmem((MEMBERS, WIDE, HEAD_DIM), jnp.float32),
            vmem((2, WIDE, CHUNK), jnp.float32),
            vmem((WIDE, ROOM), jnp.float32),
            dma((2, N_REQ - 1)),
            dma((2, 2 * MEMBERS)),
            dma((2, MEMBERS)),
            dma((2, 2 * MEMBERS)),
            dma((2, SQUARE * MEMBERS)),
            dma((2, SQUARE)),
            dma((2, MEMBERS)),
            dma((4,)),
        ],
        compiler_params=pltpu.CompilerParams(
            collective_id=0 if room == ROOM else 1, has_side_effects=True, vmem_limit_bytes=58 * 2 ** 20),
        cost_estimate=pl.CostEstimate(flops=12 * 10 ** 9, bytes_accessed=6 * 10 ** 6, transcendentals=25 * 10 ** 6),
    )(slot_owner, slot_fill, queries, stretch_kv, page_pool)


def shards(queries, stretch_kv, page_pool, slot_owner, slot_fill):
    requests = jnp.arange(N_REQ, dtype=jnp.int32)[:, None]
    tokens = jnp.sum(jnp.where(slot_owner[None] == requests, slot_fill[None], 0), axis=1)
    return lax.cond(
        jnp.max(tokens) <= ROOM, functools.partial(attend, ROOM), functools.partial(attend, PREFIX_ROWS),
        queries, stretch_kv, page_pool, slot_owner, slot_fill)


def solution(mesh):
    placed = (P("req", "ctx", None), P("req", "ctx", None), P(("req", "ctx"), None, None), P(), P())
    return jax.shard_map(
        shards, mesh=mesh, in_specs=placed, out_specs=P("req", "ctx", None), check_vma=False
    )
```

```python
import functools

import jax
import jax.numpy as jnp
from jax import lax
from jax.experimental import pallas as pl
from jax.experimental.pallas import tpu as pltpu
from jax.sharding import PartitionSpec as P

HEAD_DIM = 128
GROUP_HEADS = 8
ROWS = 128
MEMBERS = 8
SQUARE = 4
N_REQ = 4
N_CTX = 32
PAGE = 16
V_AT = 1024
CHUNK = 512
ROOM = 768
PREFIX_ROWS = 2048
WIDE = GROUP_HEADS * ROWS
Q_COLS = GROUP_HEADS * HEAD_DIM
LOW = -1e30
SCALE = HEAD_DIM ** -0.5 * 1.4426950408889634
MESH = pl.DeviceIdType.MESH
COMPUTE = True


def kernel(room, owner, fill, q_hbm, kv_hbm, pages, out_hbm, q_first, q_second, qbuf, near_kv, far_kv, pbuf, packed, page_out, page_in, obuf,
           pbias, acc, top, held, held_prefix, page_sems, gkv_sems, gq_sems, gp_sems, sq_sems, sp_sems, o_sems, own_sems):
    req = lax.axis_index("req")
    ctx = lax.axis_index("ctx")
    x, y, z = ctx // 8, (ctx // 2) % 4, ctx % 2

    def spot(square, group):
        px = x + (square % 2) * (1 - 2 * (x % 2))
        py = y + (square // 2) * (1 - 2 * (y % 2))
        px = px + (group // 4) * (3 - 2 * px)
        py = py + ((group // 2) % 2) * (3 - 2 * py)
        return px, py, z + (group % 2) * (1 - 2 * z)

    def place(square, group):
        px, py, pz = spot(square, group)
        return px * 8 + py * 2 + pz

    def head_of(group):
        px, py, pz = spot(0, group)
        return (px // 2) * 4 + (py // 2) * 2 + pz

    def cols(start, size):
        return pl.ds(pl.multiple_of(start, 128), size)

    def remote(src, dst, sems, index, ctx_to, req_to=None):
        return pltpu.make_async_remote_copy(
            src_ref=src, dst_ref=dst, send_sem=sems.at[0, index], recv_sem=sems.at[1, index],
            device_id=(req if req_to is None else req_to, ctx_to), device_id_type=MESH)

    barrier = pltpu.get_barrier_semaphore()
    for step in range(1, N_REQ):
        pl.semaphore_signal(barrier, inc=1, device_id=((req + step) % N_REQ, ctx), device_id_type=MESH)
    for group in range(1, MEMBERS):
        pl.semaphore_signal(barrier, inc=1, device_id=(req, place(0, group)), device_id_type=MESH)
    for square in (1, 2):
        pl.semaphore_signal(barrier, inc=1, device_id=(req, place(square, 0)), device_id_type=MESH)

    first_slot = (req * N_CTX + ctx) * 2
    for target in range(N_REQ):
        picked = jnp.where(owner[first_slot] == target, 0, 1)
        page_out[target] = pages[picked]
    page_in[pl.ds(req * PAGE, PAGE)] = page_out[req]
    mine = head_of(0)

    near = (1, 2, 4, 3, 5, 6, 7)

    def kv_piece(group, part):
        head = head_of(group)
        return (kv_hbm.at[0, :, cols(part * V_AT + head * HEAD_DIM, HEAD_DIM)],
                near_kv.at[0, group, :, part * HEAD_DIM:(part + 1) * HEAD_DIM])

    def q_copy(group):
        landing = q_first.at[near.index(group) + 1] if group in near[:3] else q_second.at[near.index(group) - 3]
        return remote(q_hbm.at[0, :, cols(head_of(group) * Q_COLS, Q_COLS)], landing, gq_sems, group, place(0, group))

    own_kv = [pltpu.make_async_copy(*kv_piece(0, part), own_sems.at[part]) for part in range(2)]
    own_q = pltpu.make_async_copy(q_hbm.at[0, :, cols(mine * Q_COLS, Q_COLS)], q_first.at[0], own_sems.at[2])
    for copy in own_kv:
        copy.start()
    own_q.start()
    pl.semaphore_wait(barrier, N_REQ - 1 + MEMBERS - 1 + 2)

    started = []

    def start(copy):
        copy.start()
        started.append(copy)
        return copy

    page_copies = []
    for step in range(1, N_REQ):
        target = (req + step) % N_REQ
        page_copies.append(start(remote(
            page_out.at[target], page_in.at[pl.ds(req * PAGE, PAGE)], page_sems, step - 1, ctx, target)))
    kv_copies = {0: own_kv}
    for group in near:
        kv_copies[group] = [
            start(remote(*kv_piece(group, part), gkv_sems, group * 2 + part, place(0, group)))
            for part in range(2)]
    for group in near[:3]:
        start(q_copy(group))

    for copy in page_copies:
        copy.wait_recv()
    group_pages = []
    for group in near:
        theirs = head_of(group)
        for part in range(2):
            group_pages.append(start(remote(
                page_in.at[:, cols(part * V_AT + theirs * HEAD_DIM, HEAD_DIM)],
                pbuf.at[0, group, :, part * HEAD_DIM:(part + 1) * HEAD_DIM],
                gp_sems, group * 2 + part, place(0, group))))
    for part in range(2):
        pbuf[0, 0, :, part * HEAD_DIM:(part + 1) * HEAD_DIM] = page_in[:, cols(part * V_AT + mine * HEAD_DIM, HEAD_DIM)]

    def pass_block(slot, group, bit):
        source = near_kv.at[slot // 2, group]
        target = (far_kv if bit == 1 else near_kv).at[(slot + bit) // 2, group]
        return start(remote(source, target, sq_sems, (slot + bit) * MEMBERS + group, place(bit, 0)))

    def pass_prefix(slot, bit):
        return start(remote(pbuf.at[slot], pbuf.at[slot + bit], sp_sems, slot + bit, place(bit, 0)))

    blocks = {1: [], 2: [], 3: []}
    for group in (0,) + near:
        for copy in kv_copies[group]:
            copy.wait() if group == 0 else copy.wait_recv()
        blocks[2].append(pass_block(0, group, 2))
        blocks[1].append(pass_block(0, group, 1))
    for copy in group_pages:
        copy.wait_recv()
    prefixes = {1: pass_prefix(0, 1), 2: pass_prefix(0, 2)}
    for group in near[3:]:
        start(q_copy(group))

    def product(member, keys):
        queries = jnp.concatenate(
            [qbuf[member, :, g * HEAD_DIM:(g + 1) * HEAD_DIM] for g in range(GROUP_HEADS)], axis=0)
        return lax.dot_general(queries, keys, (((1,), (1,)), ((), ())), preferred_element_type=jnp.float32)

    def weigh(scores, new, values):
        size = scores.shape[1]
        weights = jnp.exp2((scores - jnp.tile(new, (1, size // HEAD_DIM))) * SCALE).astype(jnp.bfloat16)
        ones = jnp.ones((size, HEAD_DIM), jnp.bfloat16)
        return jnp.dot(weights, jnp.concatenate([values, ones], axis=1), preferred_element_type=jnp.float32)

    def begin(member, scores, values):
        new = jnp.broadcast_to(jnp.max(scores, axis=-1, keepdims=True), (WIDE, HEAD_DIM))
        acc[member] = weigh(scores, new, values)
        top[member] = new

    def absorb(member, scores, values):
        old = top[member]
        new = jnp.maximum(old, jnp.max(scores, axis=-1, keepdims=True))
        factor = jnp.exp2((old - new) * SCALE)
        acc[member] = acc[member] * jnp.tile(factor, (1, 2)) + weigh(scores, new, values)
        top[member] = new

    def keys_of(buffer, which, half):
        return buffer[which, pl.ds(half * 4, 4), :, 0:HEAD_DIM].reshape(CHUNK, HEAD_DIM)

    def values_of(buffer, which, half):
        return buffer[which, pl.ds(half * 4, 4), :, HEAD_DIM:2 * HEAD_DIM].reshape(CHUNK, HEAD_DIM)

    def mask(scores, square, member):
        _, py, pz = spot(0, member)
        _, key_y, _ = spot(square, 0)
        lane = lax.broadcasted_iota(jnp.int32, (1, CHUNK), 1)
        from_y, from_z = lane // (2 * ROWS), (lane // ROWS) % 2
        at_y = key_y + from_y * (3 - 2 * key_y)
        at_z = z + from_z * (1 - 2 * z)
        token = (at_y * 2 + at_z - (py * 2 + pz)) * ROWS + lane % ROWS
        row = lax.broadcasted_iota(jnp.int32, (WIDE, 1), 0) % ROWS
        return jnp.where(token <= row, scores, LOW)

    def near_keys(member):
        px, py, _ = spot(0, member)
        half = member // 4
        held[0] = product(member, keys_of(near_kv, 0, half))

        @pl.when(px >= 2)
        def _():
            held[1] = product(member, keys_of(near_kv, 0, 1 - half))
            begin(member, mask(held[0], 0, member), values_of(near_kv, 0, half))
            held[0] = product(member, keys_of(near_kv, 1, half))
            absorb(member, held[1], values_of(near_kv, 0, 1 - half))
            held[1] = product(member, keys_of(near_kv, 1, 1 - half))
            absorb(member, mask(held[0], 2, member), values_of(near_kv, 1, half))
            absorb(member, held[1], values_of(near_kv, 1, 1 - half))

        @pl.when((px < 2) & (py > 0))
        def _():
            held[1] = product(member, keys_of(near_kv, 1, half))
            begin(member, mask(held[0], 0, member), values_of(near_kv, 0, half))
            absorb(member, mask(held[1], 2, member), values_of(near_kv, 1, half))

        @pl.when((px < 2) & (py == 0))
        def _():
            begin(member, mask(held[0], 0, member), values_of(near_kv, 0, half))

    def x_half():
        return spot(1, 0)[0] // 3

    row = (lax.broadcasted_iota(jnp.int32, (PAGE, HEAD_DIM), 0) * HEAD_DIM
           + lax.broadcasted_iota(jnp.int32, (PAGE, HEAD_DIM), 1))

    def count_page(index, carry):
        places, before = carry
        source = place(index // (MEMBERS * N_REQ), (index // N_REQ) % MEMBERS)
        slot = ((index % N_REQ) * N_CTX + source) * 2
        written = jnp.where(owner[slot] == req, fill[slot], jnp.where(owner[slot + 1] == req, fill[slot + 1], 0))
        token = row - index * PAGE
        inside = (token >= 0) & (token < written)
        return jnp.where(inside, token + before, places), before + written

    places, total = lax.fori_loop(0, PREFIX_ROWS // PAGE, count_page, (jnp.full_like(row, -1), jnp.int32(0)))
    pbias[...] = jnp.where(lax.broadcasted_iota(jnp.int32, (1, room), 1) < total, 0.0, LOW)

    for group, copy in zip((0,) + near, blocks[2], strict=True):
        copy.wait_recv()
        blocks[3].append(pass_block(2, group, 1))
    prefixes[1].wait_recv()
    prefixes[3] = pass_prefix(1, 2)
    own_q.wait()
    for group in near[:3]:
        q_copy(group).wait_recv()
    qbuf[0] = q_first[0]
    for group in near[:3]:
        qbuf[group] = q_first[near.index(group) + 1]

    def near_turn(turn, _):
        @pl.when(turn == 4)
        def _():
            for group in near[3:]:
                q_copy(group).wait_recv()
                qbuf[group] = q_second[near.index(group) - 3]

        late = turn // 4
        member = (1 - late) * (turn + turn // 3) + late * (turn - (7 - turn) // 3)
        if COMPUTE:
            near_keys(member)
        return 0

    lax.fori_loop(0, MEMBERS, near_turn, 0)

    prefixes[2].wait_recv()
    prefixes[3].wait_recv()
    if COMPUTE:
        for at in range(0, room, 256):
            wanted = lax.broadcasted_iota(jnp.int32, (256, HEAD_DIM), 0) + at
            chosen = jnp.concatenate(
                [jnp.where(wanted == places[k:k + 1], 1.0, 0.0).astype(jnp.bfloat16) for k in range(PAGE)], axis=1)
            packed[at:at + 256] = jnp.dot(
                chosen, pbuf[...].reshape(PREFIX_ROWS, 2 * HEAD_DIM), preferred_element_type=jnp.float32
            ).astype(jnp.bfloat16)

    for copy in blocks[1] + blocks[3]:
        copy.wait_recv()

    def out_copy(member):
        return remote(obuf.at[member], out_hbm.at[0, :, cols(mine * Q_COLS, Q_COLS)], o_sems, member, place(0, member))

    piece = ROOM if room == ROOM else CHUNK

    def prefix_scores(member, at):
        return product(member, packed[at:at + piece, 0:HEAD_DIM]) + pbias[:, at:at + piece]

    def absorb_prefix(member, at, scores):
        absorb(member, scores, packed[at:at + piece, HEAD_DIM:2 * HEAD_DIM])

    def other_keys(turn, _):
        member = MEMBERS - 1 - turn
        px, _, _ = spot(0, member)
        if COMPUTE:
            held_prefix[:, :piece] = prefix_scores(member, 0)

            @pl.when(px == 3)
            def _():
                held[0] = product(member, keys_of(far_kv, 0, 0))
                absorb_prefix(member, 0, held_prefix[:, :piece])
                held[1] = product(member, keys_of(far_kv, 0, 1))
                absorb(member, held[0], values_of(far_kv, 0, 0))
                held[0] = product(member, keys_of(far_kv, 1, 0))
                absorb(member, held[1], values_of(far_kv, 0, 1))
                held[1] = product(member, keys_of(far_kv, 1, 1))
                absorb(member, held[0], values_of(far_kv, 1, 0))
                absorb(member, held[1], values_of(far_kv, 1, 1))

            @pl.when((px == 1) | (px == 2))
            def _():
                half = x_half()
                held[0] = product(member, keys_of(far_kv, 0, half))
                absorb_prefix(member, 0, held_prefix[:, :piece])
                held[1] = product(member, keys_of(far_kv, 1, half))
                absorb(member, held[0], values_of(far_kv, 0, half))
                absorb(member, held[1], values_of(far_kv, 1, half))

            @pl.when(px == 0)
            def _():
                absorb_prefix(member, 0, held_prefix[:, :piece])

            for at in range(piece, room, piece):
                absorb_prefix(member, at, prefix_scores(member, at))
        result = (acc[member, :, :HEAD_DIM] / acc[member, :, HEAD_DIM:]).astype(jnp.bfloat16)
        for g in range(GROUP_HEADS):
            obuf[member, :, g * HEAD_DIM:(g + 1) * HEAD_DIM] = result[g * ROWS:(g + 1) * ROWS]

        @pl.when(member > 0)
        def _():
            out_copy(member).start()

        return 0

    lax.fori_loop(0, MEMBERS, other_keys, 0)
    last_copy = pltpu.make_async_copy(obuf.at[0], out_hbm.at[0, :, cols(mine * Q_COLS, Q_COLS)], own_sems.at[3])
    last_copy.start()
    for copy in started:
        copy.wait_send()
    for member in range(1, MEMBERS):
        out_copy(member).wait_recv()
        out_copy(member).wait_send()
    last_copy.wait()


def attend(room, queries, stretch_kv, page_pool, slot_owner, slot_fill):
    vmem = pltpu.VMEM
    dma = pltpu.SemaphoreType.DMA
    smem_spec = pl.BlockSpec(memory_space=pltpu.SMEM)
    any_spec = pl.BlockSpec(memory_space=pl.ANY)
    return pl.pallas_call(
        functools.partial(kernel, room),
        out_shape=jax.ShapeDtypeStruct(queries.shape, jnp.bfloat16),
        in_specs=[smem_spec, smem_spec, any_spec, any_spec, pl.BlockSpec(memory_space=vmem)],
        out_specs=any_spec,
        scratch_shapes=[
            vmem((4, ROWS, Q_COLS), jnp.bfloat16),
            vmem((4, ROWS, Q_COLS), jnp.bfloat16),
            vmem((MEMBERS, ROWS, Q_COLS), jnp.bfloat16),
            vmem((SQUARE // 2, MEMBERS, ROWS, 2 * HEAD_DIM), jnp.bfloat16),
            vmem((SQUARE // 2, MEMBERS, ROWS, 2 * HEAD_DIM), jnp.bfloat16),
            vmem((SQUARE, MEMBERS, N_REQ * PAGE, 2 * HEAD_DIM), jnp.bfloat16),
            vmem((room, 2 * HEAD_DIM), jnp.bfloat16),
            vmem((N_REQ, PAGE, 2048), jnp.bfloat16),
            vmem((N_REQ * PAGE, 2048), jnp.bfloat16),
            vmem((MEMBERS, ROWS, Q_COLS), jnp.bfloat16),
            vmem((1, room), jnp.float32),
            vmem((MEMBERS, WIDE, 2 * HEAD_DIM), jnp.float32),
            vmem((MEMBERS, WIDE, HEAD_DIM), jnp.float32),
            vmem((2, WIDE, CHUNK), jnp.float32),
            vmem((WIDE, ROOM), jnp.float32),
            dma((2, N_REQ - 1)),
            dma((2, 2 * MEMBERS)),
            dma((2, MEMBERS)),
            dma((2, 2 * MEMBERS)),
            dma((2, SQUARE * MEMBERS)),
            dma((2, SQUARE)),
            dma((2, MEMBERS)),
            dma((4,)),
        ],
        compiler_params=pltpu.CompilerParams(
            collective_id=0 if room == ROOM else 1, has_side_effects=True, vmem_limit_bytes=58 * 2 ** 20),
        cost_estimate=pl.CostEstimate(flops=12 * 10 ** 9, bytes_accessed=6 * 10 ** 6, transcendentals=25 * 10 ** 6),
    )(slot_owner, slot_fill, queries, stretch_kv, page_pool)


def shards(queries, stretch_kv, page_pool, slot_owner, slot_fill):
    requests = jnp.arange(N_REQ, dtype=jnp.int32)[:, None]
    tokens = jnp.sum(jnp.where(slot_owner[None] == requests, slot_fill[None], 0), axis=1)
    return lax.cond(
        jnp.max(tokens) <= ROOM, functools.partial(attend, ROOM), functools.partial(attend, PREFIX_ROWS),
        queries, stretch_kv, page_pool, slot_owner, slot_fill)


def solution(mesh):
    placed = (P("req", "ctx", None), P("req", "ctx", None), P(("req", "ctx"), None, None), P(), P())
    return jax.shard_map(
        shards, mesh=mesh, in_specs=placed, out_specs=P("req", "ctx", None), check_vma=False
    )
```
